256 devices in a mesh: dp: 16 (over y, z_hi), latent: 16 (over z_lo, x, core).
Axes of the slice: x: 4, y: 4, z: 8 (z_hi: 4, z_lo: 2; z = z_hi * 2 + z_lo), core: 2. Of those that a mesh axis runs over, the one named last changes fastest.
Arguments:
- activations: bfloat16 [8192, 3584], P('dp'), may hold values from -6 to 6
- w_enc: float32 [3584, 8192], P('dp', 'latent'), may hold values from -0.09375 to 0.09375
- w_dec: float32 [3584, 8192], P('dp', 'latent'), may hold values from -0.0625 to 0.0625
- b_enc: float32 [8192], P('latent'), may hold values from -3 to 3
- b_dec: float32 [3584], replicated, may hold values from -3 to 3
- m_enc: float32 [3584, 8192], P('dp', 'latent'), may hold values from -0.12 to 0.12
- v_enc: float32 [3584, 8192], P('dp', 'latent'), may hold values from 0.0001 to 0.001
- m_dec: float32 [3584, 8192], P('dp', 'latent'), may hold values from -0.12 to 0.12
- v_dec: float32 [3584, 8192], P('dp', 'latent'), may hold values from 0.0001 to 0.001
- m_b_enc: float32 [8192], P('latent'), may hold values from -0.12 to 0.12
- v_b_enc: float32 [8192], P('latent'), may hold values from 0.0001 to 0.001
- m_b_dec: float32 [3584], replicated, may hold values from -0.12 to 0.12
- v_b_dec: float32 [3584], replicated, may hold values from 0.0001 to 0.001
Outputs:
- new_w_enc: float32 [3584, 8192], P('dp', 'latent')
- new_m_enc: float32 [3584, 8192], P('dp', 'latent')
- new_v_enc: float32 [3584, 8192], P('dp', 'latent')
- new_w_dec: float32 [3584, 8192], P('dp', 'latent')
- new_m_dec: float32 [3584, 8192], P('dp', 'latent')
- new_v_dec: float32 [3584, 8192], P('dp', 'latent')
- new_b_enc: float32 [8192], P('latent')
- new_m_b_enc: float32 [8192], P('latent')
- new_v_b_enc: float32 [8192], P('latent')
- new_b_dec: float32 [3584], replicated
- new_m_b_dec: float32 [3584], replicated
- new_v_b_dec: float32 [3584], replicated
The draws below stay inside these ranges and needn't reach their ends.
All inputs are finite; a program needn't handle non-finite values.
Results may differ from the reference program's by a relative error of at most 0.0082.
Values may be sent and summed in bfloat16 or wider, within the bound.
No kernel may reach another device: no remote copies, remote signals or barrier semaphores. Data moves between devices by JAX's collectives and lax.ppermute only.
A program may use at most 128 MiB of HBM per device.

```python
import math
import jax
import jax.numpy as jnp
from jax import lax

D = 3584
ADAM_STEP = 100
LAT = 8192
ROWS = 8192


def shard_levels(stream_key, extent, shards, least, high):
    factor_of = 1.0
    for position, blocks in shards:
        draws = jax.random.uniform(jax.random.fold_in(jax.random.fold_in(stream_key, 6), position), (blocks,), jnp.float32, least / len(shards), high / len(shards))
        factor_of = factor_of * jnp.repeat(jnp.exp(draws), extent[position] // blocks).reshape((-1,) + (1,) * (len(extent) - 1 - position))
    return factor_of


def normal_values(key, shape, width, bound, pieces=(), held_as=jnp.bfloat16):
    array = width * jax.random.normal(key, shape, jnp.float32)
    if pieces:
        array = array * shard_levels(key, shape, pieces, -0.22, 0.18)
    return jnp.clip(array, -bound, bound).astype(held_as)


def setup_inputs(seed: int = 0) -> dict:
    key_list = jax.random.split(jax.random.key(seed), 14)
    activations = normal_values(key_list[0], (ROWS, D), 1.0, 6.0, ((0, 16),))
    w_enc = normal_values(key_list[1], (D, LAT), D ** -0.5, 0.09375, ((0, 16), (1, 16)), jnp.float32)
    w_dec = normal_values(key_list[2], (D, LAT), LAT ** -0.5, 0.0625, ((0, 16), (1, 16)), jnp.float32)
    b_enc = normal_values(key_list[3], (LAT,), 0.5, 3.0, ((0, 16),), jnp.float32)
    b_dec = normal_values(key_list[4], (D,), 0.5, 3.0, (), jnp.float32)
    m_enc = normal_values(key_list[5], (D, LAT), 0.02, 0.12, ((0, 16), (1, 16)), jnp.float32)
    v_enc = jnp.clip(jnp.exp(math.log(0.001) - 2.3025852 * jax.random.uniform(key_list[6], (D, LAT), jnp.float32) ** shard_levels(key_list[6], (D, LAT), ((0, 16), (1, 16)), -0.2, 0.2)), 0.0001, 0.001)
    m_dec = normal_values(key_list[7], (D, LAT), 0.02, 0.12, ((0, 16), (1, 16)), jnp.float32)
    v_dec = jnp.clip(jnp.exp(math.log(0.001) - 2.3025852 * jax.random.uniform(key_list[8], (D, LAT), jnp.float32) ** shard_levels(key_list[8], (D, LAT), ((0, 16), (1, 16)), -0.2, 0.2)), 0.0001, 0.001)
    m_b_enc = normal_values(key_list[9], (LAT,), 0.02, 0.12, ((0, 16),), jnp.float32)
    v_b_enc = jnp.clip(jnp.exp(math.log(0.001) - 2.3025852 * jax.random.uniform(key_list[10], (LAT,), jnp.float32) ** shard_levels(key_list[10], (LAT,), ((0, 16),), -0.2, 0.2)), 0.0001, 0.001)
    m_b_dec = normal_values(key_list[11], (D,), 0.02, 0.12, (), jnp.float32)
    v_b_dec = jnp.clip(jnp.exp(jax.random.uniform(key_list[12], (D,), jnp.float32, math.log(0.0001), math.log(0.001))), 0.0001, 0.001)
    return dict(activations=activations, w_enc=w_enc, w_dec=w_dec, b_enc=b_enc, b_dec=b_dec, m_enc=m_enc, v_enc=v_enc, m_dec=m_dec, v_dec=v_dec, m_b_enc=m_b_enc, v_b_enc=v_b_enc, m_b_dec=m_b_dec, v_b_dec=v_b_dec)


BETA_ONE = 0.9
BETA_TWO = 0.999
LEARNING_RATE = 0.001
ADAM_EPS = 1e-08
NORM_EPS = 1e-06
SPARSITY = 5.0

def adam_step(weights, gradient, moment_one, moment_two):
    one_new = BETA_ONE * moment_one + (1.0 - BETA_ONE) * gradient
    two_new = BETA_TWO * moment_two + (1.0 - BETA_TWO) * gradient * gradient
    fix_one = 1.0 - BETA_ONE ** ADAM_STEP
    fix_two = 1.0 - BETA_TWO ** ADAM_STEP
    updated = weights - LEARNING_RATE * (one_new / fix_one) / (jnp.sqrt(two_new / fix_two) + ADAM_EPS)
    return (updated, one_new, two_new)

def contract_rows(left, right):
    return lax.dot_general(left, right, (((0,), (0,)), ((), ())), preferred_element_type=jnp.float32)

def reference(activations, w_enc, w_dec, b_enc, b_dec, m_enc, v_enc, m_dec, v_dec, m_b_enc, v_b_enc, m_b_dec, v_b_dec):
    enc_half = w_enc.astype(jnp.bfloat16)
    dec_half = w_dec.astype(jnp.bfloat16)
    preacts = jnp.dot(activations, enc_half, preferred_element_type=jnp.float32) + b_enc
    features = jnp.maximum(preacts, 0.0).astype(jnp.bfloat16)
    dec_wide = dec_half.astype(jnp.float32)
    col_norms = jnp.sqrt(lax.optimization_barrier(jnp.sum(dec_wide * dec_wide, axis=0)) + NORM_EPS)
    rebuilt = lax.dot_general(features, dec_half, (((1,), (1,)), ((), ())), preferred_element_type=jnp.float32) + b_dec
    scaling = 2.0 / ROWS
    grad_out = ((rebuilt - activations.astype(jnp.float32)) * scaling).astype(jnp.bfloat16)
    grad_feat = jnp.dot(grad_out, dec_half, preferred_element_type=jnp.float32) + SPARSITY / ROWS * col_norms
    grad_pre = jnp.where(preacts > 0.0, grad_feat, 0.0).astype(jnp.bfloat16)
    totals = lax.optimization_barrier(jnp.sum(features.astype(jnp.float32), axis=0))
    grad_w_enc = contract_rows(activations, grad_pre)
    grad_w_dec = contract_rows(grad_out, features) + SPARSITY / ROWS * (totals / col_norms) * dec_wide
    grad_b_enc = lax.optimization_barrier(jnp.sum(grad_pre.astype(jnp.float32), axis=0))
    grad_b_dec = lax.optimization_barrier(jnp.sum(grad_out.astype(jnp.float32), axis=0))
    new_w_enc, new_m_enc, new_v_enc = adam_step(w_enc, grad_w_enc, m_enc, v_enc)
    new_w_dec, new_m_dec, new_v_dec = adam_step(w_dec, grad_w_dec, m_dec, v_dec)
    new_b_enc, new_m_b_enc, new_v_b_enc = adam_step(b_enc, grad_b_enc, m_b_enc, v_b_enc)
    new_b_dec, new_m_b_dec, new_v_b_dec = adam_step(b_dec, grad_b_dec, m_b_dec, v_b_dec)
    return (new_w_enc, new_m_enc, new_v_enc, new_w_dec, new_m_dec, new_v_dec, new_b_enc, new_m_b_enc, new_v_b_enc, new_b_dec, new_m_b_dec, new_v_b_dec)
```

```python
import jax
import jax.numpy as jnp
from jax import lax
from jax.sharding import PartitionSpec as P

ADAM_STEP = 100


BETA_ONE = 0.9
BETA_TWO = 0.999
LEARNING_RATE = 0.001
ADAM_EPS = 1e-08
NORM_EPS = 1e-06
SPARSITY = 5.0

HALF = jnp.bfloat16
WIDE = jnp.float32

Y, Z = 4, 4
GROUPS = 8


def adam_step(weights, gradient, moment_one, moment_two):
    one_new = BETA_ONE * moment_one + (1.0 - BETA_ONE) * gradient
    two_new = BETA_TWO * moment_two + (1.0 - BETA_TWO) * gradient * gradient
    fix_one = 1.0 - BETA_ONE**ADAM_STEP
    fix_two = 1.0 - BETA_TWO**ADAM_STEP
    updated = weights - LEARNING_RATE * (one_new / fix_one) / (
        jnp.sqrt(two_new / fix_two) + ADAM_EPS
    )
    return (updated, one_new, two_new)


def dot(left, right, left_dim, right_dim):
    return lax.dot_general(
        left, right, (((left_dim,), (right_dim,)), ((), ())), preferred_element_type=WIDE
    )


def send_y(x, step):
    return lax.ppermute(x, "dp", [(s, (s // Z + step) % Y * Z + s % Z) for s in range(Y * Z)])


def send_z(x, step):
    return lax.ppermute(x, "dp", [(s, s // Z * Z + (s % Z + step) % Z) for s in range(Y * Z)])


def swap_core(x):
    return lax.ppermute(x, "latent", [(s, s ^ 1) for s in range(2 * GROUPS)])


def to_groups(x):
    return lax.all_to_all(
        x,
        "latent",
        split_axis=0,
        concat_axis=0,
        tiled=True,
        axis_index_groups=[[c + 2 * g for g in range(GROUPS)] for c in range(2)],
    )


def rows_at(x, start, count):
    return lax.dynamic_slice_in_dim(x, start, count, axis=0)


def put_rows(x, part, start):
    return lax.dynamic_update_slice_in_dim(x, part, start, axis=0)


def split_wide(x):
    high = lax.reduce_precision(x, 8, 7)
    return high.astype(HALF), (x - high).astype(HALF)


def body(
    activations,
    w_enc,
    w_dec,
    b_enc,
    b_dec,
    m_enc,
    v_enc,
    m_dec,
    v_dec,
    m_b_enc,
    v_b_enc,
    m_b_dec,
    v_b_dec,
):
    group_rows, width = activations.shape
    rows_total = group_rows * Y * Z
    own_rows, lat_width = w_enc.shape
    y_rows = own_rows * Z
    core_rows = width // 2
    slice_rows = core_rows // GROUPS
    dp_at, lat_at = lax.axis_index("dp"), lax.axis_index("latent")
    y_at, z_at = dp_at // Z, dp_at % Z
    group_at, core_at = lat_at // 2, lat_at % 2
    scaling = 2.0 / rows_total
    penalty = SPARSITY / rows_total

    def y_off(step):
        return (y_at + step) % Y * y_rows

    def z_off(step):
        return (z_at + step) % Z * own_rows

    enc_half = w_enc.astype(HALF)
    dec_half = w_dec.astype(HALF)
    dec_full = lax.all_gather(dec_half, "dp", axis=0, tiled=True)

    block = jnp.zeros((y_rows, lat_width), HALF)
    block = put_rows(block, enc_half, z_off(0))
    for step in (1, -1, 2):
        block = put_rows(block, send_z(enc_half, -step), z_off(step))
    blocks = {0: block}
    for step in (1, -1, 2):
        blocks[step] = send_y(block, -step)
    preacts = b_enc[None, :]
    for step in (0, 1, -1, 2):
        part = lax.dynamic_slice_in_dim(activations, y_off(step), y_rows, axis=1)
        preacts = preacts + dot(part, blocks[step], 1, 0)
    features = jnp.maximum(preacts, 0.0).astype(HALF)
    act_t = activations.T

    mine, other = core_at * core_rows, (1 - core_at) * core_rows
    dec_mine, dec_other = rows_at(dec_full, mine, core_rows), rows_at(dec_full, other, core_rows)
    away = swap_core(dot(dec_other, features, 1, 1).astype(HALF))
    pair = (dot(dec_mine, features, 1, 1) + away.astype(WIDE)).astype(HALF)
    parts = to_groups(pair).reshape(GROUPS, slice_rows, group_rows)
    rebuilt = jnp.sum(parts.astype(WIDE), axis=0)
    at = mine + group_at * slice_rows
    bias = lax.dynamic_slice_in_dim(b_dec, at, slice_rows)[:, None]
    out_slice = (
        (rebuilt + bias - rows_at(act_t, at, slice_rows).astype(WIDE)) * scaling
    ).astype(HALF)
    out_mine = to_groups(
        jnp.broadcast_to(out_slice[None], (GROUPS, slice_rows, group_rows)).reshape(
            core_rows, group_rows
        )
    )
    out_other = swap_core(out_mine)

    dec_wide = dec_full.astype(WIDE)
    col_norms = jnp.sqrt(jnp.sum(dec_wide * dec_wide, axis=0) + NORM_EPS)
    totals = jnp.sum(features.astype(WIDE), axis=0)
    weighted = penalty * totals / col_norms

    grad_feat = dot(out_mine, dec_mine, 0, 0) + penalty * col_norms
    grad_feat = grad_feat + dot(out_other, dec_other, 0, 0)
    grad_pre = jnp.where(preacts > 0.0, grad_feat, 0.0).astype(HALF)
    out_t = put_rows(jnp.zeros((width, group_rows), HALF), out_mine, mine)
    out_t = put_rows(out_t, out_other, other)

    bias_parts = jnp.concatenate(
        [
            jnp.sum(grad_pre.astype(WIDE), axis=0),
            jnp.sum(out_t.astype(WIDE), axis=1),
        ]
    ).reshape(-1, lat_width)
    bias_rows = bias_parts.shape[0]

    def dec_block(step):
        at = y_off(step)
        return dot(rows_at(out_t, at, y_rows), features, 1, 0) + weighted * rows_at(
            dec_full, at, y_rows
        ).astype(WIDE)

    def enc_block(step):
        return dot(rows_at(act_t, y_off(step), y_rows), grad_pre, 1, 0)

    def with_bias(x, sums):
        return jnp.concatenate([x.astype(HALF), *split_wide(sums)], axis=0)

    def unpack(x):
        x = x.astype(WIDE)
        n = x.shape[0] - 2 * bias_rows
        return x[:n], x[n : n + bias_rows] + x[n + bias_rows :]

    dec_sum = dec_block(0)
    for step in (1, -1, 2):
        dec_sum = dec_sum + send_y(dec_block(step).astype(HALF), step).astype(WIDE)
    grad_w_dec = rows_at(dec_sum, z_off(0), own_rows)
    for step in (1, -1, 2):
        piece = rows_at(dec_sum, z_off(step), own_rows).astype(HALF)
        grad_w_dec = grad_w_dec + send_z(piece, step).astype(WIDE)

    enc_sum, bias_sum = enc_block(0), bias_parts
    for step in (1, -1, 2):
        got, sums = unpack(send_y(with_bias(enc_block(step), bias_parts), step))
        enc_sum, bias_sum = enc_sum + got, bias_sum + sums
    grad_w_enc, bias_all = rows_at(enc_sum, z_off(0), own_rows), bias_sum
    for step in (1, -1, 2):
        piece = rows_at(enc_sum, z_off(step), own_rows)
        got, sums = unpack(send_z(with_bias(piece, bias_sum), step))
        grad_w_enc, bias_all = grad_w_enc + got, bias_all + sums
    bias_all = bias_all.reshape(-1)
    grad_b_enc, grad_b_dec = bias_all[:lat_width], bias_all[lat_width:]

    new_w_enc, new_m_enc, new_v_enc = adam_step(w_enc, grad_w_enc, m_enc, v_enc)
    new_w_dec, new_m_dec, new_v_dec = adam_step(w_dec, grad_w_dec, m_dec, v_dec)
    new_b_enc, new_m_b_enc, new_v_b_enc = adam_step(b_enc, grad_b_enc, m_b_enc, v_b_enc)
    new_b_dec, new_m_b_dec, new_v_b_dec = adam_step(b_dec, grad_b_dec, m_b_dec, v_b_dec)
    return (
        new_w_enc,
        new_m_enc,
        new_v_enc,
        new_w_dec,
        new_m_dec,
        new_v_dec,
        new_b_enc,
        new_m_b_enc,
        new_v_b_enc,
        new_b_dec,
        new_m_b_dec,
        new_v_b_dec,
    )


def solution(mesh):
    full, lat, rep = P("dp", "latent"), P("latent"), P()
    in_specs = (P("dp", None), full, full, lat, rep, full, full, full, full, lat, lat, rep, rep)
    out_specs = (full, full, full, full, full, full, lat, lat, lat, rep, rep, rep)
    return jax.shard_map(body, mesh=mesh, in_specs=in_specs, out_specs=out_specs, check_vma=False)
```

```python
import jax
import jax.numpy as jnp
from jax import lax
from jax.experimental import pallas as pl
from jax.experimental.pallas import tpu as pltpu
from jax.sharding import PartitionSpec as P

ADAM_STEP = 100


BETA_ONE = 0.9
BETA_TWO = 0.999
LEARNING_RATE = 0.001
ADAM_EPS = 1e-08
NORM_EPS = 1e-06
SPARSITY = 5.0

HALF = jnp.bfloat16
WIDE = jnp.float32

Y, Z = 4, 4
GROUPS = 8


def adam_step(weights, gradient, moment_one, moment_two):
    one_new = BETA_ONE * moment_one + (1.0 - BETA_ONE) * gradient
    two_new = BETA_TWO * moment_two + (1.0 - BETA_TWO) * gradient * gradient
    fix_one = 1.0 - BETA_ONE**ADAM_STEP
    fix_two = 1.0 - BETA_TWO**ADAM_STEP
    updated = weights - LEARNING_RATE * (one_new / fix_one) / (
        jnp.sqrt(two_new / fix_two) + ADAM_EPS
    )
    return (updated, one_new, two_new)


def dot(left, right, left_dim, right_dim):
    return lax.dot_general(
        left, right, (((left_dim,), (right_dim,)), ((), ())), preferred_element_type=WIDE
    )


def send_y(x, step):
    return lax.ppermute(x, "dp", [(s, (s // Z + step) % Y * Z + s % Z) for s in range(Y * Z)])


def send_z(x, step):
    return lax.ppermute(x, "dp", [(s, s // Z * Z + (s % Z + step) % Z) for s in range(Y * Z)])


def swap_core(x):
    return lax.ppermute(x, "latent", [(s, s ^ 1) for s in range(2 * GROUPS)])


def to_groups(x):
    return lax.all_to_all(
        x,
        "latent",
        split_axis=0,
        concat_axis=0,
        tiled=True,
        axis_index_groups=[[c + 2 * g for g in range(GROUPS)] for c in range(2)],
    )


def rows_at(x, start, count):
    return lax.dynamic_slice_in_dim(x, start, count, axis=0)


def put_rows(x, part, start):
    return lax.dynamic_update_slice_in_dim(x, part, start, axis=0)


def ring_gather(x, send):
    half = half_rows(x)
    near, back = send(x, -1), send(x, 1)
    return {0: [x], 1: [near], -1: [back], 2: [send(near[:half], -1), send(back[half:], 1)]}


def half_rows(x):
    return x.shape[0] // 32 * 16


def split_wide(x):
    high = lax.reduce_precision(x, 8, 7)
    return high.astype(HALF), (x - high).astype(HALF)


def feature_grads(out_t, dec_full, start, preacts, block_rows):
    rows, lats = preacts.shape
    steps = out_t.shape[0] // block_rows

    def kernel(out_ref, dec_ref, start_ref, preacts_ref, feat_ref, sums_ref, lat_ref, total):
        step = pl.program_id(0)

        @pl.when(step == 0)
        def _():
            total[...] = jnp.broadcast_to(start_ref[...], total.shape)

        out = out_ref[...]
        total[...] += dot(out, dec_ref[...], 0, 0)
        sums_ref[...] = dot(jnp.ones((8, rows), HALF), out, 1, 1)

        @pl.when(step == steps - 1)
        def _():
            feat = jnp.where(preacts_ref[...] > 0.0, total[...], 0.0).astype(HALF)
            lat_ref[...] = dot(jnp.ones((8, rows), HALF), feat, 1, 0)
            feat_ref[...] = feat

    return pl.pallas_call(
        kernel,
        grid=(steps,),
        in_specs=[
            pl.BlockSpec((block_rows, rows), lambda i: (i, 0)),
            pl.BlockSpec((block_rows, lats), lambda i: (i, 0)),
            pl.BlockSpec((1, lats), lambda i: (0, 0)),
            pl.BlockSpec((rows, lats), lambda i: (0, 0)),
        ],
        out_specs=[
            pl.BlockSpec((rows, lats), lambda i: (0, 0)),
            pl.BlockSpec((8, block_rows), lambda i: (0, i)),
            pl.BlockSpec((8, lats), lambda i: (0, 0)),
        ],
        out_shape=[
            jax.ShapeDtypeStruct((rows, lats), HALF),
            jax.ShapeDtypeStruct((8, out_t.shape[0]), WIDE),
            jax.ShapeDtypeStruct((8, lats), WIDE),
        ],
        scratch_shapes=[pltpu.VMEM((rows, lats), WIDE)],
        compiler_params=pltpu.CompilerParams(
            dimension_semantics=("arbitrary",), vmem_limit_bytes=24 * 1024 * 1024
        ),
        cost_estimate=pl.CostEstimate(
            flops=rows * lats * block_rows, bytes_accessed=rows * lats, transcendentals=0
        ),
    )(out_t, dec_full, start, preacts)


def far_block(at, act_t, grad_pre, sums, half):
    rows, lats = grad_pre.shape
    extra = 2 * sums.shape[0]

    def kernel(at_ref, act_ref, grad_ref, sums_ref, one_ref, two_ref):
        part = dot(act_ref[...], grad_ref[...], 1, 0).astype(HALF)

        @pl.when(pl.program_id(0) == 0)
        def _():
            one_ref[0:half, :] = part
            total = sums_ref[...]
            high = total.astype(HALF).astype(WIDE)
            one_ref[half:, :] = jnp.concatenate([high, total - high], axis=0).astype(HALF)

        @pl.when(pl.program_id(0) == 1)
        def _():
            two_ref[...] = part

    return pl.pallas_call(
        kernel,
        grid_spec=pltpu.PrefetchScalarGridSpec(
            num_scalar_prefetch=1,
            grid=(2,),
            in_specs=[
                pl.BlockSpec((half, rows), lambda i, at: (at[0] + i, 0)),
                pl.BlockSpec((rows, lats), lambda i, at: (0, 0)),
                pl.BlockSpec(sums.shape, lambda i, at: (0, 0)),
            ],
            out_specs=[
                pl.BlockSpec((half + extra, lats), lambda i, at: (0, 0)),
                pl.BlockSpec((half, lats), lambda i, at: (0, 0)),
            ],
        ),
        out_shape=[
            jax.ShapeDtypeStruct((half + extra, lats), HALF),
            jax.ShapeDtypeStruct((half, lats), HALF),
        ],
        compiler_params=pltpu.CompilerParams(
            dimension_semantics=("arbitrary",), vmem_limit_bytes=24 * 1024 * 1024
        ),
        cost_estimate=pl.CostEstimate(
            flops=rows * lats * half, bytes_accessed=rows * lats, transcendentals=0
        ),
    )(at.reshape(1), act_t, grad_pre, sums)


def body(
    activations,
    w_enc,
    w_dec,
    b_enc,
    b_dec,
    m_enc,
    v_enc,
    m_dec,
    v_dec,
    m_b_enc,
    v_b_enc,
    m_b_dec,
    v_b_dec,
):
    group_rows, width = activations.shape
    rows_total = group_rows * Y * Z
    own_rows, lat_width = w_enc.shape
    y_rows = own_rows * Z
    core_rows = width // 2
    slice_rows = core_rows // GROUPS
    dp_at, lat_at = lax.axis_index("dp"), lax.axis_index("latent")
    y_at, z_at = dp_at >> 2, dp_at & 3
    group_at, core_at = lat_at >> 1, lat_at & 1
    scaling = 2.0 / rows_total
    penalty = SPARSITY / rows_total

    def y_off(step):
        return (y_at + step & 3) * y_rows

    def z_off(step):
        return (z_at + step & 3) * own_rows

    enc_half = w_enc.astype(HALF)
    dec_half = w_dec.astype(HALF)
    dec_full = lax.all_gather(dec_half, "dp", axis=0, tiled=True)

    act_t = activations.T
    along_z = ring_gather(enc_half, send_z)
    own_z = ring_gather(enc_half, send_y)
    other_z = ring_gather(jnp.concatenate(along_z[1] + along_z[-1] + along_z[2], axis=0), send_y)
    preacts = b_enc[None, :]

    def add_dots(preacts, left, pieces):
        at = 0
        for piece in pieces:
            preacts = preacts + dot(left[at : at + piece.shape[0]], piece, 0, 0)
            at += piece.shape[0]
        return preacts

    for step in (0, 1, -1, 2):
        left = rows_at(act_t, y_off(step) + z_off(0), own_rows)
        preacts = add_dots(preacts, left, own_z[step])
    for step in (0, 1, -1, 2):
        left = jnp.concatenate(
            [rows_at(act_t, y_off(step) + z_off(k), own_rows) for k in (1, -1, 2)], axis=0
        )
        preacts = add_dots(preacts, left, other_z[step])
    features = jnp.maximum(preacts, 0.0).astype(HALF)

    mine, other = core_at * core_rows, (1 - core_at) * core_rows
    dec_mine, dec_other = rows_at(dec_full, mine, core_rows), rows_at(dec_full, other, core_rows)
    away = swap_core(dot(dec_other, features, 1, 1).astype(HALF))
    kept = lax.optimization_barrier(dot(dec_mine, features, 1, 1))
    pair = (kept + away.astype(WIDE)).astype(HALF)
    parts = to_groups(pair).reshape(GROUPS, slice_rows, group_rows)

    dec_wide = dec_full.astype(WIDE)
    col_norms = jnp.sqrt(jnp.sum(dec_wide * dec_wide, axis=0) + NORM_EPS)
    totals = jnp.sum(features.astype(WIDE), axis=0)
    weighted = penalty * totals / col_norms
    parts, col_norms, weighted = lax.optimization_barrier((parts, col_norms, weighted))

    rebuilt = jnp.sum(parts.astype(WIDE), axis=0)
    at = mine + group_at * slice_rows
    bias = lax.dynamic_slice_in_dim(b_dec, at, slice_rows)[:, None]
    out_slice = (
        (rebuilt + bias - rows_at(act_t, at, slice_rows).astype(WIDE)) * scaling
    ).astype(HALF)
    out_mine = to_groups(
        jnp.broadcast_to(out_slice[None], (GROUPS, slice_rows, group_rows)).reshape(
            core_rows, group_rows
        )
    )
    out_other = swap_core(out_mine)

    half = y_rows // 2
    fix = lax.optimization_barrier

    def with_bias(x, sums):
        return jnp.concatenate([x.astype(HALF), *split_wide(sums)], axis=0)

    def unpack(x):
        x = x.astype(WIDE)
        n = x.shape[0] - 2 * bias_rows
        return x[:n], x[n : n + bias_rows] + x[n + bias_rows :]

    def joined(block, part, at):
        rest = block.shape[0] - part.shape[0] - at
        return block.astype(WIDE) + jnp.pad(part.astype(WIDE), ((at, rest), (0, 0)))

    out_t = put_rows(jnp.zeros((width, group_rows), HALF), out_mine, mine)
    out_t = put_rows(fix(out_t), out_other, other)

    def dec_rows(step, at, count, tied=()):
        at = y_off(step) + at
        out = fix((rows_at(out_t, at, count), *tied))[0]
        return dot(out, features, 1, 0) + weighted * rows_at(dec_full, at, count).astype(WIDE)

    far = [dec_rows(2, 0, half).astype(HALF), dec_rows(2, half, half).astype(HALF)]
    dec_far = [send_y(far[0], 1), send_y(far[1], -1)]

    late = fix((out_t, *far))[0]
    grad_pre, sums, lat_sums = feature_grads(
        late, dec_full, penalty * col_norms[None], preacts, y_rows
    )

    bias_parts = jnp.concatenate([lat_sums[0], sums[0]]).reshape(-1, lat_width)
    bias_rows = bias_parts.shape[0]

    def enc_rows(step, at, count):
        return dot(rows_at(act_t, y_off(step) + at, count), grad_pre, 1, 0)

    far = far_block((y_at + 2 & 3) * 2, act_t, grad_pre, bias_parts, half)
    enc_far = [send_y(far[0], 1), send_y(far[1], -1)]

    near = fix(dec_rows(1, 0, y_rows, far).astype(HALF))
    back = fix(dec_rows(-1, 0, y_rows, far).astype(HALF))
    dec_near = send_y(joined(near, dec_far[0], 0).astype(HALF), 1)
    dec_back = send_y(joined(back, dec_far[1], half).astype(HALF), -1)
    near = fix(enc_rows(1, 0, y_rows).astype(HALF))
    back = fix(enc_rows(-1, 0, y_rows).astype(HALF))
    got, sums = unpack(enc_far[0])
    enc_near = send_y(with_bias(joined(near, got, 0), bias_parts + sums), 1)
    enc_back = send_y(with_bias(joined(back, enc_far[1], half), bias_parts), -1)

    def z_rows(step, *blocks):
        return sum(rows_at(block, z_off(step), own_rows).astype(WIDE) for block in blocks)

    blocks = (fix(dec_rows(0, 0, y_rows, far).astype(HALF)), dec_near, dec_back)
    pieces = [z_rows(step, *blocks).astype(HALF) for step in (2, 1, -1)]
    grad_w_dec = z_rows(0, *blocks)
    for piece, step in zip(pieces, (2, 1, -1)):
        grad_w_dec = grad_w_dec + send_z(piece, step).astype(WIDE)
    enc_own = fix((fix(enc_rows(0, 0, y_rows).astype(HALF)), *pieces))[0]

    blocks = (enc_own, enc_near, enc_back)
    bias_sum = bias_parts + unpack(enc_near)[1] + unpack(enc_back)[1]
    grad_w_enc, bias_all = z_rows(0, *blocks), bias_sum
    for step in (2, 1, -1):
        got, sums = unpack(send_z(with_bias(z_rows(step, *blocks), bias_sum), step))
        grad_w_enc, bias_all = grad_w_enc + got, bias_all + sums
    bias_all = bias_all.reshape(-1)
    grad_b_enc, grad_b_dec = bias_all[:lat_width], bias_all[lat_width:]

    new_w_enc, new_m_enc, new_v_enc = adam_step(w_enc, grad_w_enc, m_enc, v_enc)
    new_w_dec, new_m_dec, new_v_dec = adam_step(w_dec, grad_w_dec, m_dec, v_dec)
    new_b_enc, new_m_b_enc, new_v_b_enc = adam_step(b_enc, grad_b_enc, m_b_enc, v_b_enc)
    new_b_dec, new_m_b_dec, new_v_b_dec = adam_step(b_dec, grad_b_dec, m_b_dec, v_b_dec)
    return (
        new_w_enc,
        new_m_enc,
        new_v_enc,
        new_w_dec,
        new_m_dec,
        new_v_dec,
        new_b_enc,
        new_m_b_enc,
        new_v_b_enc,
        new_b_dec,
        new_m_b_dec,
        new_v_b_dec,
    )


def solution(mesh):
    full, lat, rep = P("dp", "latent"), P("latent"), P()
    in_specs = (P("dp", None), full, full, lat, rep, full, full, full, full, lat, lat, rep, rep)
    out_specs = (full, full, full, full, full, full, lat, lat, lat, rep, rep, rep)
    return jax.shard_map(body, mesh=mesh, in_specs=in_specs, out_specs=out_specs, check_vma=False)
```

```python
import jax
import jax.numpy as jnp
from jax import lax
from jax.experimental import pallas as pl
from jax.experimental.pallas import tpu as pltpu
from jax.sharding import PartitionSpec as P

ADAM_STEP = 100


BETA_ONE = 0.9
BETA_TWO = 0.999
LEARNING_RATE = 0.001
ADAM_EPS = 1e-08
NORM_EPS = 1e-06
SPARSITY = 5.0

HALF = jnp.bfloat16
WIDE = jnp.float32

Y, Z = 4, 4
GROUPS = 8


def adam_step(weights, gradient, moment_one, moment_two):
    one_new = BETA_ONE * moment_one + (1.0 - BETA_ONE) * gradient
    two_new = BETA_TWO * moment_two + (1.0 - BETA_TWO) * gradient * gradient
    fix_one = 1.0 - BETA_ONE**ADAM_STEP
    fix_two = 1.0 - BETA_TWO**ADAM_STEP
    updated = weights - LEARNING_RATE * (one_new / fix_one) / (
        jnp.sqrt(two_new / fix_two) + ADAM_EPS
    )
    return (updated, one_new, two_new)


def dot(left, right, left_dim, right_dim):
    return lax.dot_general(
        left, right, (((left_dim,), (right_dim,)), ((), ())), preferred_element_type=WIDE
    )


def send_y(x, step):
    return lax.ppermute(x, "dp", [(s, (s // Z + step) % Y * Z + s % Z) for s in range(Y * Z)])


def send_z(x, step):
    return lax.ppermute(x, "dp", [(s, s // Z * Z + (s % Z + step) % Z) for s in range(Y * Z)])


def swap_core(x):
    return lax.ppermute(x, "latent", [(s, s ^ 1) for s in range(2 * GROUPS)])


def to_groups(x):
    return lax.all_to_all(
        x,
        "latent",
        split_axis=0,
        concat_axis=0,
        tiled=True,
        axis_index_groups=[[c + 2 * g for g in range(GROUPS)] for c in range(2)],
    )


def rows_at(x, start, count):
    return lax.dynamic_slice_in_dim(x, start, count, axis=0)


def put_rows(x, part, start):
    return lax.dynamic_update_slice_in_dim(x, part, start, axis=0)


def ring_gather(x, send):
    half = half_rows(x)
    near, back = send(x, -1), send(x, 1)
    return {0: [x], 1: [near], -1: [back], 2: [send(near[:half], -1), send(back[half:], 1)]}


def half_rows(x):
    return x.shape[0] // 32 * 16


def split_wide(x):
    high = lax.reduce_precision(x, 8, 7)
    return high.astype(HALF), (x - high).astype(HALF)


def feature_grads(out_t, dec_full, start, preacts, block_rows):
    rows, lats = preacts.shape
    steps = out_t.shape[0] // block_rows

    def kernel(out_ref, dec_ref, start_ref, preacts_ref, feat_ref, sums_ref, lat_ref, total):
        step = pl.program_id(0)

        @pl.when(step == 0)
        def _():
            total[...] = jnp.broadcast_to(start_ref[...], total.shape)

        out = out_ref[...]
        total[...] += dot(out, dec_ref[...], 0, 0)
        sums_ref[...] = dot(jnp.ones((8, rows), HALF), out, 1, 1)

        @pl.when(step == steps - 1)
        def _():
            feat = jnp.where(preacts_ref[...] > 0.0, total[...], 0.0).astype(HALF)
            lat_ref[...] = dot(jnp.ones((8, rows), HALF), feat, 1, 0)
            feat_ref[...] = feat

    return pl.pallas_call(
        kernel,
        grid=(steps,),
        in_specs=[
            pl.BlockSpec((block_rows, rows), lambda i: (i, 0)),
            pl.BlockSpec((block_rows, lats), lambda i: (i, 0)),
            pl.BlockSpec((1, lats), lambda i: (0, 0)),
            pl.BlockSpec((rows, lats), lambda i: (0, 0)),
        ],
        out_specs=[
            pl.BlockSpec((rows, lats), lambda i: (0, 0)),
            pl.BlockSpec((8, block_rows), lambda i: (0, i)),
            pl.BlockSpec((8, lats), lambda i: (0, 0)),
        ],
        out_shape=[
            jax.ShapeDtypeStruct((rows, lats), HALF),
            jax.ShapeDtypeStruct((8, out_t.shape[0]), WIDE),
            jax.ShapeDtypeStruct((8, lats), WIDE),
        ],
        scratch_shapes=[pltpu.VMEM((rows, lats), WIDE)],
        compiler_params=pltpu.CompilerParams(
            dimension_semantics=("arbitrary",), vmem_limit_bytes=24 * 1024 * 1024
        ),
        cost_estimate=pl.CostEstimate(
            flops=rows * lats * block_rows, bytes_accessed=rows * lats, transcendentals=0
        ),
    )(out_t, dec_full, start, preacts)


def far_block(at, act_t, grad_pre, sums, half):
    rows, lats = grad_pre.shape
    extra = 2 * sums.shape[0]

    def kernel(at_ref, act_ref, grad_ref, sums_ref, one_ref, two_ref):
        part = dot(act_ref[...], grad_ref[...], 1, 0).astype(HALF)

        @pl.when(pl.program_id(0) == 0)
        def _():
            one_ref[0:half, :] = part
            total = sums_ref[...]
            high = total.astype(HALF).astype(WIDE)
            one_ref[half:, :] = jnp.concatenate([high, total - high], axis=0).astype(HALF)

        @pl.when(pl.program_id(0) == 1)
        def _():
            two_ref[...] = part

    return pl.pallas_call(
        kernel,
        grid_spec=pltpu.PrefetchScalarGridSpec(
            num_scalar_prefetch=1,
            grid=(2,),
            in_specs=[
                pl.BlockSpec((half, rows), lambda i, at: (at[0] + i, 0)),
                pl.BlockSpec((rows, lats), lambda i, at: (0, 0)),
                pl.BlockSpec(sums.shape, lambda i, at: (0, 0)),
            ],
            out_specs=[
                pl.BlockSpec((half + extra, lats), lambda i, at: (0, 0)),
                pl.BlockSpec((half, lats), lambda i, at: (0, 0)),
            ],
        ),
        out_shape=[
            jax.ShapeDtypeStruct((half + extra, lats), HALF),
            jax.ShapeDtypeStruct((half, lats), HALF),
        ],
        compiler_params=pltpu.CompilerParams(
            dimension_semantics=("arbitrary",), vmem_limit_bytes=24 * 1024 * 1024
        ),
        cost_estimate=pl.CostEstimate(
            flops=rows * lats * half, bytes_accessed=rows * lats, transcendentals=0
        ),
    )(at.reshape(1), act_t, grad_pre, sums)


def body(
    activations,
    w_enc,
    w_dec,
    b_enc,
    b_dec,
    m_enc,
    v_enc,
    m_dec,
    v_dec,
    m_b_enc,
    v_b_enc,
    m_b_dec,
    v_b_dec,
):
    group_rows, width = activations.shape
    rows_total = group_rows * Y * Z
    own_rows, lat_width = w_enc.shape
    y_rows = own_rows * Z
    core_rows = width // 2
    slice_rows = core_rows // GROUPS
    piece_rows = own_rows // 2
    dp_at, lat_at = lax.axis_index("dp"), lax.axis_index("latent")
    y_at, z_at = dp_at >> 2, dp_at & 3
    group_at, core_at = lat_at >> 1, lat_at & 1
    scaling = 2.0 / rows_total
    penalty = SPARSITY / rows_total

    def y_off(step):
        return (y_at + step & 3) * y_rows

    def z_off(step):
        return (z_at + step & 3) * own_rows

    enc_half = w_enc.astype(HALF)
    dec_half = w_dec.astype(HALF)

    def by_core(own, away, axis):
        return jnp.where(
            core_at == 0,
            jnp.concatenate([own, away], axis=axis),
            jnp.concatenate([away, own], axis=axis),
        )

    dec_away = swap_core(rows_at(dec_half, (1 - core_at) * piece_rows, piece_rows))
    dec_pair = by_core(rows_at(dec_half, core_at * piece_rows, piece_rows), dec_away, 1)
    dec_rows_own = lax.all_gather(dec_pair, "dp", axis=0, tiled=True)

    def by_rows(own, away):
        shape = (Y * Z, 1, piece_rows, own.shape[1])
        both = jnp.zeros((Y * Z, 2, piece_rows, own.shape[1]), own.dtype)
        for part, core in ((own, core_at), (away, 1 - core_at)):
            at = (0, core, 0, 0)
            both = lax.dynamic_update_slice(both, part.reshape(shape), at)
        return both.reshape(width, -1)


    act_t = activations.T
    along_z = ring_gather(enc_half, send_z)
    own_z = ring_gather(enc_half, send_y)
    other_z = ring_gather(jnp.concatenate(along_z[1] + along_z[-1] + along_z[2], axis=0), send_y)
    preacts = b_enc[None, :]

    def add_dots(preacts, left, pieces):
        at = 0
        for piece in pieces:
            preacts = preacts + dot(left[at : at + piece.shape[0]], piece, 0, 0)
            at += piece.shape[0]
        return preacts

    for step in (0, 1, -1, 2):
        left = rows_at(act_t, y_off(step) + z_off(0), own_rows)
        preacts = add_dots(preacts, left, own_z[step])
    for step in (0, 1, -1, 2):
        left = jnp.concatenate(
            [rows_at(act_t, y_off(step) + z_off(k), own_rows) for k in (1, -1, 2)], axis=0
        )
        preacts = add_dots(preacts, left, other_z[step])
    features = jnp.maximum(preacts, 0.0).astype(HALF)

    both = by_core(features, swap_core(features), 1)
    pair = dot(dec_rows_own, both, 1, 1).astype(HALF)
    parts = to_groups(pair).reshape(GROUPS, slice_rows, group_rows)

    gathered = lax.optimization_barrier((dec_rows_own, pair))[0]
    sides = gathered[:, :lat_width], gathered[:, lat_width:]
    dec_full = by_rows(
        jnp.where(core_at == 0, *sides), swap_core(jnp.where(core_at == 0, *sides[::-1]))
    )
    dec_wide = dec_full.astype(WIDE)
    col_norms = jnp.sqrt(jnp.sum(dec_wide * dec_wide, axis=0) + NORM_EPS)
    totals = jnp.sum(features.astype(WIDE), axis=0)
    weighted = penalty * totals / col_norms
    parts, dec_full, col_norms, weighted = lax.optimization_barrier(
        (parts, dec_full, col_norms, weighted)
    )

    rebuilt = jnp.sum(parts.astype(WIDE), axis=0)
    at = (group_at, 0, core_at, 0)
    bias = lax.dynamic_slice(
        b_dec.reshape(GROUPS, 2, 2, piece_rows), at, (1, 2, 1, piece_rows)
    ).reshape(slice_rows, 1)
    target = lax.dynamic_slice(
        act_t.reshape(GROUPS, 2, 2, piece_rows, group_rows),
        (*at, 0),
        (1, 2, 1, piece_rows, group_rows),
    ).reshape(slice_rows, group_rows)
    out_slice = ((rebuilt + bias - target.astype(WIDE)) * scaling).astype(HALF)
    out_mine = to_groups(
        jnp.broadcast_to(out_slice[None], (GROUPS, slice_rows, group_rows)).reshape(
            core_rows, group_rows
        )
    )
    out_other = swap_core(out_mine)

    half = y_rows // 2
    fix = lax.optimization_barrier

    def with_bias(x, sums):
        return jnp.concatenate([x.astype(HALF), *split_wide(sums)], axis=0)

    def unpack(x):
        x = x.astype(WIDE)
        n = x.shape[0] - 2 * bias_rows
        return x[:n], x[n : n + bias_rows] + x[n + bias_rows :]

    def joined(block, part, at):
        rest = block.shape[0] - part.shape[0] - at
        return block.astype(WIDE) + jnp.pad(part.astype(WIDE), ((at, rest), (0, 0)))

    out_t = by_rows(out_mine, out_other)

    def dec_rows(step, at, count, tied=()):
        at = y_off(step) + at
        out = fix((rows_at(out_t, at, count), *tied))[0]
        return dot(out, features, 1, 0) + weighted * rows_at(dec_full, at, count).astype(WIDE)

    far = [dec_rows(2, 0, half).astype(HALF), dec_rows(2, half, half).astype(HALF)]
    dec_far = [send_y(far[0], 1), send_y(far[1], -1)]

    late = fix((out_t, *far))[0]
    grad_pre, sums, lat_sums = feature_grads(
        late, dec_full, penalty * col_norms[None], preacts, y_rows
    )

    bias_parts = jnp.concatenate([lat_sums[0], sums[0]]).reshape(-1, lat_width)
    bias_rows = bias_parts.shape[0]

    def enc_rows(step, at, count):
        return dot(rows_at(act_t, y_off(step) + at, count), grad_pre, 1, 0)

    far = far_block((y_at + 2 & 3) * 2, act_t, grad_pre, bias_parts, half)
    enc_far = [send_y(far[0], 1), send_y(far[1], -1)]

    near = fix(dec_rows(1, 0, y_rows, far).astype(HALF))
    back = fix(dec_rows(-1, 0, y_rows, far).astype(HALF))
    dec_near = send_y(joined(near, dec_far[0], 0).astype(HALF), 1)
    dec_back = send_y(joined(back, dec_far[1], half).astype(HALF), -1)
    near = fix(enc_rows(1, 0, y_rows).astype(HALF))
    back = fix(enc_rows(-1, 0, y_rows).astype(HALF))
    got, sums = unpack(enc_far[0])
    enc_near = send_y(with_bias(joined(near, got, 0), bias_parts + sums), 1)
    enc_back = send_y(with_bias(joined(back, enc_far[1], half), bias_parts), -1)

    def z_rows(step, *blocks):
        return sum(rows_at(block, z_off(step), own_rows).astype(WIDE) for block in blocks)

    blocks = (fix(dec_rows(0, 0, y_rows, far).astype(HALF)), dec_near, dec_back)
    pieces = [z_rows(step, *blocks).astype(HALF) for step in (2, 1, -1)]
    grad_w_dec = z_rows(0, *blocks)
    for piece, step in zip(pieces, (2, 1, -1)):
        grad_w_dec = grad_w_dec + send_z(piece, step).astype(WIDE)
    enc_own = fix((fix(enc_rows(0, 0, y_rows).astype(HALF)), *pieces))[0]

    blocks = (enc_own, enc_near, enc_back)
    bias_sum = bias_parts + unpack(enc_near)[1] + unpack(enc_back)[1]
    grad_w_enc, bias_all = z_rows(0, *blocks), bias_sum
    for step in (2, 1, -1):
        got, sums = unpack(send_z(with_bias(z_rows(step, *blocks), bias_sum), step))
        grad_w_enc, bias_all = grad_w_enc + got, bias_all + sums
    bias_all = bias_all.reshape(-1)
    grad_b_enc, grad_b_dec = bias_all[:lat_width], bias_all[lat_width:]

    new_w_enc, new_m_enc, new_v_enc = adam_step(w_enc, grad_w_enc, m_enc, v_enc)
    new_w_dec, new_m_dec, new_v_dec = adam_step(w_dec, grad_w_dec, m_dec, v_dec)
    new_b_enc, new_m_b_enc, new_v_b_enc = adam_step(b_enc, grad_b_enc, m_b_enc, v_b_enc)
    new_b_dec, new_m_b_dec, new_v_b_dec = adam_step(b_dec, grad_b_dec, m_b_dec, v_b_dec)
    return (
        new_w_enc,
        new_m_enc,
        new_v_enc,
        new_w_dec,
        new_m_dec,
        new_v_dec,
        new_b_enc,
        new_m_b_enc,
        new_v_b_enc,
        new_b_dec,
        new_m_b_dec,
        new_v_b_dec,
    )


def solution(mesh):
    full, lat, rep = P("dp", "latent"), P("latent"), P()
    in_specs = (P("dp", None), full, full, lat, rep, full, full, full, full, lat, lat, rep, rep)
    out_specs = (full, full, full, full, full, full, lat, lat, lat, rep, rep, rep)
    return jax.shard_map(body, mesh=mesh, in_specs=in_specs, out_specs=out_specs, check_vma=False)
```

```python
import jax
import jax.numpy as jnp
from jax import lax
from jax.experimental import pallas as pl
from jax.experimental.pallas import tpu as pltpu
from jax.sharding import PartitionSpec as P

ADAM_STEP = 100


BETA_ONE = 0.9
BETA_TWO = 0.999
LEARNING_RATE = 0.001
ADAM_EPS = 1e-08
NORM_EPS = 1e-06
SPARSITY = 5.0

HALF = jnp.bfloat16
WIDE = jnp.float32

Y, Z = 4, 4
GROUPS = 8


def adam_step(weights, gradient, moment_one, moment_two):
    one_new = BETA_ONE * moment_one + (1.0 - BETA_ONE) * gradient
    two_new = BETA_TWO * moment_two + (1.0 - BETA_TWO) * gradient * gradient
    fix_one = 1.0 - BETA_ONE**ADAM_STEP
    fix_two = 1.0 - BETA_TWO**ADAM_STEP
    updated = weights - LEARNING_RATE * (one_new / fix_one) / (
        jnp.sqrt(two_new / fix_two) + ADAM_EPS
    )
    return (updated, one_new, two_new)


def dot(left, right, left_dim, right_dim):
    return lax.dot_general(
        left, right, (((left_dim,), (right_dim,)), ((), ())), preferred_element_type=WIDE
    )


def send_y(x, step):
    return lax.ppermute(x, "dp", [(s, (s // Z + step) % Y * Z + s % Z) for s in range(Y * Z)])


def send_z(x, step):
    return lax.ppermute(x, "dp", [(s, s // Z * Z + (s % Z + step) % Z) for s in range(Y * Z)])


def swap_core(x):
    return lax.ppermute(x, "latent", [(s, s ^ 1) for s in range(2 * GROUPS)])


def to_groups(x):
    return lax.all_to_all(
        x,
        "latent",
        split_axis=0,
        concat_axis=0,
        tiled=True,
        axis_index_groups=[[c + 2 * g for g in range(GROUPS)] for c in range(2)],
    )


def rows_at(x, start, count):
    return lax.dynamic_slice_in_dim(x, start, count, axis=0)


def put_rows(x, part, start):
    return lax.dynamic_update_slice_in_dim(x, part, start, axis=0)


def ring_gather(x, send):
    half = half_rows(x)
    near, back = send(x, -1), send(x, 1)
    return {0: [x], 1: [near], -1: [back], 2: [send(near[:half], -1), send(back[half:], 1)]}


def half_rows(x):
    return x.shape[0] // 32 * 16


def split_wide(x):
    high = lax.reduce_precision(x, 8, 7)
    return high.astype(HALF), (x - high).astype(HALF)


def feature_grads(out_t, dec_full, start, preacts, block_rows):
    rows, lats = preacts.shape
    steps = out_t.shape[0] // block_rows

    def kernel(out_ref, dec_ref, start_ref, preacts_ref, feat_ref, sums_ref, lat_ref, total):
        step = pl.program_id(0)

        @pl.when(step == 0)
        def _():
            total[...] = jnp.broadcast_to(start_ref[...], total.shape)

        out = out_ref[...]
        total[...] += dot(out, dec_ref[...], 0, 0)
        sums_ref[...] = dot(jnp.ones((8, rows), HALF), out, 1, 1)

        @pl.when(step == steps - 1)
        def _():
            feat = jnp.where(preacts_ref[...] > 0.0, total[...], 0.0).astype(HALF)
            lat_ref[...] = dot(jnp.ones((8, rows), HALF), feat, 1, 0)
            feat_ref[...] = feat

    return pl.pallas_call(
        kernel,
        grid=(steps,),
        in_specs=[
            pl.BlockSpec((block_rows, rows), lambda i: (i, 0)),
            pl.BlockSpec((block_rows, lats), lambda i: (i, 0)),
            pl.BlockSpec((1, lats), lambda i: (0, 0)),
            pl.BlockSpec((rows, lats), lambda i: (0, 0)),
        ],
        out_specs=[
            pl.BlockSpec((rows, lats), lambda i: (0, 0)),
            pl.BlockSpec((8, block_rows), lambda i: (0, i)),
            pl.BlockSpec((8, lats), lambda i: (0, 0)),
        ],
        out_shape=[
            jax.ShapeDtypeStruct((rows, lats), HALF),
            jax.ShapeDtypeStruct((8, out_t.shape[0]), WIDE),
            jax.ShapeDtypeStruct((8, lats), WIDE),
        ],
        scratch_shapes=[pltpu.VMEM((rows, lats), WIDE)],
        compiler_params=pltpu.CompilerParams(
            dimension_semantics=("arbitrary",), vmem_limit_bytes=24 * 1024 * 1024
        ),
        cost_estimate=pl.CostEstimate(
            flops=rows * lats * block_rows, bytes_accessed=rows * lats, transcendentals=0
        ),
    )(out_t, dec_full, start, preacts)


def far_block(at, act_t, grad_pre, sums, half):
    rows, lats = grad_pre.shape
    extra = 2 * sums.shape[0]

    def kernel(at_ref, act_ref, grad_ref, sums_ref, one_ref, two_ref):
        part = dot(act_ref[...], grad_ref[...], 1, 0).astype(HALF)

        @pl.when(pl.program_id(0) == 0)
        def _():
            one_ref[0:half, :] = part
            total = sums_ref[...]
            high = total.astype(HALF).astype(WIDE)
            one_ref[half:, :] = jnp.concatenate([high, total - high], axis=0).astype(HALF)

        @pl.when(pl.program_id(0) == 1)
        def _():
            two_ref[...] = part

    return pl.pallas_call(
        kernel,
        grid_spec=pltpu.PrefetchScalarGridSpec(
            num_scalar_prefetch=1,
            grid=(2,),
            in_specs=[
                pl.BlockSpec((half, rows), lambda i, at: (at[0] + i, 0)),
                pl.BlockSpec((rows, lats), lambda i, at: (0, 0)),
                pl.BlockSpec(sums.shape, lambda i, at: (0, 0)),
            ],
            out_specs=[
                pl.BlockSpec((half + extra, lats), lambda i, at: (0, 0)),
                pl.BlockSpec((half, lats), lambda i, at: (0, 0)),
            ],
        ),
        out_shape=[
            jax.ShapeDtypeStruct((half + extra, lats), HALF),
            jax.ShapeDtypeStruct((half, lats), HALF),
        ],
        compiler_params=pltpu.CompilerParams(
            dimension_semantics=("arbitrary",), vmem_limit_bytes=24 * 1024 * 1024
        ),
        cost_estimate=pl.CostEstimate(
            flops=rows * lats * half, bytes_accessed=rows * lats, transcendentals=0
        ),
    )(at.reshape(1), act_t, grad_pre, sums)


def body(
    activations,
    w_enc,
    w_dec,
    b_enc,
    b_dec,
    m_enc,
    v_enc,
    m_dec,
    v_dec,
    m_b_enc,
    v_b_enc,
    m_b_dec,
    v_b_dec,
):
    group_rows, width = activations.shape
    rows_total = group_rows * Y * Z
    own_rows, lat_width = w_enc.shape
    y_rows = own_rows * Z
    core_rows = width // 2
    slice_rows = core_rows // GROUPS
    piece_rows = own_rows // 2
    dp_at, lat_at = lax.axis_index("dp"), lax.axis_index("latent")
    y_at, z_at = dp_at >> 2, dp_at & 3
    group_at, core_at = lat_at >> 1, lat_at & 1
    scaling = 2.0 / rows_total
    penalty = SPARSITY / rows_total

    def y_off(step):
        return (y_at + step & 3) * y_rows

    def z_off(step):
        return (z_at + step & 3) * own_rows

    enc_half = w_enc.astype(HALF)
    dec_half = w_dec.astype(HALF)

    def by_core(own, away, axis):
        return jnp.where(
            core_at == 0,
            jnp.concatenate([own, away], axis=axis),
            jnp.concatenate([away, own], axis=axis),
        )

    dec_away = swap_core(rows_at(dec_half, (1 - core_at) * piece_rows, piece_rows))
    dec_pair = by_core(rows_at(dec_half, core_at * piece_rows, piece_rows), dec_away, 1)
    dec_rows_own = lax.all_gather(dec_pair, "dp", axis=0, tiled=True)

    def by_rows(own, away):
        shape = (Y * Z, 1, piece_rows, own.shape[1])
        both = jnp.zeros((Y * Z, 2, piece_rows, own.shape[1]), own.dtype)
        for part, core in ((own, core_at), (away, 1 - core_at)):
            at = (0, core, 0, 0)
            both = lax.dynamic_update_slice(both, part.reshape(shape), at)
        return both.reshape(width, -1)


    act_t = activations.T
    along_z = ring_gather(enc_half, send_z)
    own_z = ring_gather(enc_half, send_y)
    other_z = ring_gather(jnp.concatenate(along_z[1] + along_z[-1] + along_z[2], axis=0), send_y)
    preacts = b_enc[None, :]

    def add_dots(preacts, left, pieces):
        at = 0
        for piece in pieces:
            preacts = preacts + dot(left[at : at + piece.shape[0]], piece, 0, 0)
            at += piece.shape[0]
        return preacts

    for step in (0, 1, -1, 2):
        left = rows_at(act_t, y_off(step) + z_off(0), own_rows)
        preacts = add_dots(preacts, left, own_z[step])
    for step in (0, 1, -1, 2):
        left = jnp.concatenate(
            [rows_at(act_t, y_off(step) + z_off(k), own_rows) for k in (1, -1, 2)], axis=0
        )
        preacts = add_dots(preacts, left, other_z[step])
    features = jnp.maximum(preacts, 0.0).astype(HALF)

    both = by_core(features, swap_core(features), 1)
    pair = dot(dec_rows_own, both, 1, 1).astype(HALF)
    parts = to_groups(pair).reshape(GROUPS, slice_rows, group_rows)

    gathered = lax.optimization_barrier((dec_rows_own, pair))[0]
    sides = gathered[:, :lat_width], gathered[:, lat_width:]
    dec_full = by_rows(
        jnp.where(core_at == 0, *sides), swap_core(jnp.where(core_at == 0, *sides[::-1]))
    )
    dec_wide = dec_full.astype(WIDE)
    col_norms = jnp.sqrt(jnp.sum(dec_wide * dec_wide, axis=0) + NORM_EPS)
    totals = jnp.sum(features.astype(WIDE), axis=0)
    weighted = penalty * totals / col_norms
    parts, dec_full, col_norms, weighted = lax.optimization_barrier(
        (parts, dec_full, col_norms, weighted)
    )

    rebuilt = jnp.sum(parts.astype(WIDE), axis=0)
    at = (group_at, 0, core_at, 0)
    bias = lax.dynamic_slice(
        b_dec.reshape(GROUPS, 2, 2, piece_rows), at, (1, 2, 1, piece_rows)
    ).reshape(slice_rows, 1)
    target = lax.dynamic_slice(
        act_t.reshape(GROUPS, 2, 2, piece_rows, group_rows),
        (*at, 0),
        (1, 2, 1, piece_rows, group_rows),
    ).reshape(slice_rows, group_rows)
    out_slice = ((rebuilt + bias - target.astype(WIDE)) * scaling).astype(HALF)
    out_mine = to_groups(
        jnp.broadcast_to(out_slice[None], (GROUPS, slice_rows, group_rows)).reshape(
            core_rows, group_rows
        )
    )
    out_other = swap_core(out_mine)

    half = y_rows // 2
    fix = lax.optimization_barrier

    def with_bias(x, sums):
        return jnp.concatenate([x.astype(HALF), *split_wide(sums)], axis=0)

    def unpack(x):
        x = x.astype(WIDE)
        n = x.shape[0] - 2 * bias_rows
        return x[:n], x[n : n + bias_rows] + x[n + bias_rows :]

    def joined(block, part, at):
        rest = block.shape[0] - part.shape[0] - at
        return block.astype(WIDE) + jnp.pad(part.astype(WIDE), ((at, rest), (0, 0)))

    out_t = by_rows(out_mine, out_other)

    def dec_rows(step, at, count, tied=()):
        at = y_off(step) + at
        out = fix((rows_at(out_t, at, count), *tied))[0]
        return dot(out, features, 1, 0) + weighted * rows_at(dec_full, at, count).astype(WIDE)

    far = [dec_rows(2, 0, half).astype(HALF), dec_rows(2, half, half).astype(HALF)]
    dec_far = [send_y(far[0], 1), send_y(far[1], -1)]

    late = fix((out_t, *far))[0]
    grad_pre, sums, lat_sums = feature_grads(
        late, dec_full, penalty * col_norms[None], preacts, y_rows
    )

    bias_parts = jnp.concatenate([lat_sums[0], sums[0]]).reshape(-1, lat_width)
    bias_rows = bias_parts.shape[0]

    def enc_rows(step, at, count):
        return dot(rows_at(act_t, y_off(step) + at, count), grad_pre, 1, 0)

    far = far_block((y_at + 2 & 3) * 2, act_t, grad_pre, bias_parts, half)
    enc_far = [send_y(far[0], 1), send_y(far[1], -1)]

    near = fix(dec_rows(1, 0, y_rows, far).astype(HALF))
    back = fix(dec_rows(-1, 0, y_rows, far).astype(HALF))
    dec_near = send_y(joined(near, dec_far[0], 0).astype(HALF), 1)
    dec_back = send_y(joined(back, dec_far[1], half).astype(HALF), -1)
    near = fix(enc_rows(1, 0, y_rows).astype(HALF))
    back = fix(enc_rows(-1, 0, y_rows).astype(HALF))
    got, sums = unpack(enc_far[0])
    enc_near = send_y(with_bias(joined(near, got, 0), bias_parts + sums), 1)
    enc_back = send_y(with_bias(joined(back, enc_far[1], half), bias_parts), -1)

    def z_rows(step, *blocks):
        return sum(rows_at(block, z_off(step), own_rows).astype(WIDE) for block in blocks)

    blocks = (fix(dec_rows(0, 0, y_rows, far).astype(HALF)), dec_near, dec_back)
    pieces = [z_rows(step, *blocks).astype(HALF) for step in (1, -1, 2)]
    grad_w_dec = z_rows(0, *blocks)
    for piece, step in zip(pieces, (1, -1, 2)):
        grad_w_dec = grad_w_dec + send_z(piece, step).astype(WIDE)
    enc_own = fix((fix(enc_rows(0, 0, y_rows).astype(HALF)), *pieces))[0]

    blocks = (enc_own, enc_near, enc_back)
    bias_sum = bias_parts + unpack(enc_near)[1] + unpack(enc_back)[1]
    grad_w_enc, bias_all = z_rows(0, *blocks), bias_sum
    for step in (1, -1, 2):
        got, sums = unpack(send_z(with_bias(z_rows(step, *blocks), bias_sum), step))
        grad_w_enc, bias_all = grad_w_enc + got, bias_all + sums
    bias_all = bias_all.reshape(-1)
    grad_b_enc, grad_b_dec = bias_all[:lat_width], bias_all[lat_width:]

    new_w_enc, new_m_enc, new_v_enc = adam_step(w_enc, grad_w_enc, m_enc, v_enc)
    new_w_dec, new_m_dec, new_v_dec = adam_step(w_dec, grad_w_dec, m_dec, v_dec)
    new_b_enc, new_m_b_enc, new_v_b_enc = adam_step(b_enc, grad_b_enc, m_b_enc, v_b_enc)
    new_b_dec, new_m_b_dec, new_v_b_dec = adam_step(b_dec, grad_b_dec, m_b_dec, v_b_dec)
    return (
        new_w_enc,
        new_m_enc,
        new_v_enc,
        new_w_dec,
        new_m_dec,
        new_v_dec,
        new_b_enc,
        new_m_b_enc,
        new_v_b_enc,
        new_b_dec,
        new_m_b_dec,
        new_v_b_dec,
    )


def solution(mesh):
    full, lat, rep = P("dp", "latent"), P("latent"), P()
    in_specs = (P("dp", None), full, full, lat, rep, full, full, full, full, lat, lat, rep, rep)
    out_specs = (full, full, full, full, full, full, lat, lat, lat, rep, rep, rep)
    return jax.shard_map(body, mesh=mesh, in_specs=in_specs, out_specs=out_specs, check_vma=False)
```
